128 devices in a mesh: area: 8 (over x, core), sub: 16 (over z, y).
Axes of the slice: x: 4, y: 4, z: 4, core: 2. Of those that a mesh axis runs over, the one named last changes fastest.
Arguments:
- blocks: float32 [8, 1024, 64, 256], P('area', 'sub'), as said below
- pattern: int32 [8, 1024, 4], P('area', 'sub'), may hold values from 0 to 1023, as said below
- line_ends: int32 [8, 2, 64], P('area'), may hold values from 0 to 65535, as said below
- sources: float32 [4, 8, 65536], P(None, 'area', 'sub'), may hold values from -6 to 6
- capacity: float32 [8, 65536], P('area', 'sub'), may hold values from 0.2 to 2
- start_volt: float32 [8, 65536], P('area', 'sub'), may hold values from -6 to 6
- start_hist: float32 [8, 2, 64], P('area'), may hold values from -6 to 6
- surge: float32 [8, 64], P('area'), may hold values from 0.2 to 1
Outputs:
- volt: float32 [8, 65536], P('area', 'sub')
- hist: float32 [8, 2, 64], P('area')
The draws below stay inside these ranges and needn't reach their ends.
Inputs may be any that keep to these rules, and one draw needn't show every extreme that they name: pattern[a, r, 0] = r. Split the 1024 block rows of an area into aligned groups of 64: the other entries of a row never point into the row's own group, no two of them in one group are equal, and the entries of one group point into between 12 and 13 distinct block rows of each other group, exactly 13 for some group. `line_ends`: within an area the line-end buses are distinct and rise from the first left end to the last right end. `blocks`: the diagonal of each first stored block lies in 2 to 4.
All inputs are finite; a program needn't handle non-finite values.
Results may differ from the reference program's by a relative error of at most 0.00011.
Values sent between devices are 32-bit elements; how exact they have to be, the bound alone decides.
A program may use at most 64 MiB of HBM per device.

```python
import math
import jax
import jax.numpy as jnp
from jax import lax

BR_DEV = 64
BLOCK = 64
NNZ = 4
LB = 64
STEPS = 4
SWEEPS = 8
AREAS = 8
NB = 1024
BUSES = 65536


def draw_blocks(key, part):
    key_off, key_diag = jax.random.split(key)
    shape = (AREAS, NB, BLOCK, NNZ * BLOCK)
    offdiag = 0.17 * jax.random.normal(key_off, shape, jnp.float32)
    diagonal = jax.random.uniform(key_diag, (AREAS, NB, BLOCK, 1), jnp.float32, 2.0, 4.0)
    marker = jnp.arange(BLOCK)[:, None] == jnp.arange(NNZ * BLOCK)[None, :]
    return jnp.where(marker, diagonal, offdiag)


def draw_pattern(key, part):
    groups = NB // BR_DEV
    slots = BR_DEV * (NNZ - 1)
    key_slots, key_shift, key_pool = jax.random.split(key, 3)
    slot_scores = jax.random.randint(key_slots, (AREAS, groups, slots), 0, 1 << 16, dtype=jnp.int32)
    slot_scores = slot_scores * slots + jnp.arange(slots, dtype=jnp.int32)
    slot_order = jnp.argsort(slot_scores, axis=-1).astype(jnp.int32)
    shift_amount = jax.random.randint(key_shift, (AREAS, groups, 1), 0, groups - 1, dtype=jnp.int32)
    residue = (slot_order + shift_amount) % (groups - 1)
    rank_in_source = slot_order // (groups - 1)
    own_group = jnp.arange(groups, dtype=jnp.int32)[None, :, None]
    source_group = (own_group + 1 + residue) % groups
    pool_scores = jax.random.randint(key_pool, (AREAS, groups, groups, BR_DEV), 0, 1 << 16, dtype=jnp.int32)
    pool_scores = pool_scores * BR_DEV + jnp.arange(BR_DEV, dtype=jnp.int32)
    pool_order = jnp.argsort(pool_scores, axis=-1).astype(jnp.int32)
    flat_pool = pool_order.reshape(AREAS, groups, groups * BR_DEV)
    local_pick = jnp.take_along_axis(flat_pool, source_group * BR_DEV + rank_in_source, axis=2)
    column = source_group * BR_DEV + local_pick
    others = column.reshape(AREAS, NB, NNZ - 1)
    rowids = jnp.arange(NB, dtype=jnp.int32)
    first = jnp.broadcast_to(rowids[None, :, None], (AREAS, NB, 1))
    return jnp.concatenate([first, others], axis=2).astype(jnp.int32)


def draw_line_ends(key, part):
    stride = BUSES // (2 * LB)
    base = jnp.arange(2 * LB, dtype=jnp.int32) * stride
    offsets = jax.random.randint(key, (AREAS, 2 * LB), 0, stride, dtype=jnp.int32)
    chosen = base[None, :] + offsets
    chosen = chosen.at[0, 0].set(0)
    chosen = chosen.at[0, 2 * LB - 1].set(BUSES - 1)
    return chosen.reshape(AREAS, 2, LB).astype(jnp.int32)


def block_scale(own_key, shape, shards, low, largest):
    factor_of = 1.0
    for axis_at, shards_of in shards:
        draws = jax.random.uniform(jax.random.fold_in(jax.random.fold_in(own_key, 6), axis_at), (shards_of,), jnp.float32, low / len(shards), largest / len(shards))
        factor_of = factor_of * jnp.repeat(jnp.exp(draws), shape[axis_at] // shards_of).reshape((-1,) + (1,) * (len(shape) - 1 - axis_at))
    return factor_of


def noise(stream_key, shape, spread, most, shards=(), kind=jnp.bfloat16):
    factor_of = block_scale(stream_key, shape, shards, -0.22, 0.18) if shards else 1.0
    entries = jax.random.normal(stream_key, shape, jnp.float32) * spread * factor_of
    return jnp.minimum(jnp.maximum(entries, -most), most).astype(kind)


def setup_inputs(seed: int = 0) -> dict:
    splits = jax.random.split(jax.random.key(seed), 9)
    blocks = draw_blocks(jax.random.fold_in(splits[8], 71), 0)
    pattern = draw_pattern(jax.random.fold_in(splits[8], 71), 0)
    line_ends = draw_line_ends(jax.random.fold_in(splits[8], 71), 0)
    sources = noise(splits[3], (STEPS, AREAS, BUSES), 1.0, 6.0, ((1, 8), (2, 16)), jnp.float32)
    capacity = jnp.clip(jnp.exp(math.log(2.0) - 2.3025851 * jax.random.uniform(splits[4], (AREAS, BUSES), jnp.float32) ** block_scale(splits[4], (AREAS, BUSES), ((0, 8), (1, 16)), -0.2, 0.2)), 0.2, 2.0)
    start_volt = noise(splits[5], (AREAS, BUSES), 1.0, 6.0, ((0, 8), (1, 16)), jnp.float32)
    start_hist = noise(splits[6], (AREAS, 2, LB), 1.0, 6.0, ((0, 8),), jnp.float32)
    surge = jnp.clip(jnp.exp(math.log(1.0) - 1.609438 * jax.random.uniform(splits[7], (AREAS, LB), jnp.float32) ** block_scale(splits[7], (AREAS, LB), ((0, 8),), -0.2, 0.2)), 0.2, 1.0)
    return {"blocks": blocks, "pattern": pattern, "line_ends": line_ends, "sources": sources, "capacity": capacity, "start_volt": start_volt, "start_hist": start_hist, "surge": surge}


def product(blocks, pattern, field):
    areas = field.shape[0]
    width = blocks.shape[2]
    nblk = blocks.shape[1]
    field_blocks = field.reshape(areas, nblk, width)
    picked = jax.vmap(lambda xa, pa: xa[pa])(field_blocks, pattern)
    picked = picked.reshape(areas, nblk, -1)
    result = jnp.einsum("arik,ark->ari", blocks, picked, precision=lax.Precision.HIGHEST)
    return result.reshape(areas, -1)


def reference(blocks, pattern, line_ends, sources, capacity, start_volt, start_hist, surge):
    areas = start_volt.shape[0]
    width = blocks.shape[2]
    diag = jnp.diagonal(blocks[..., :width], axis1=2, axis2=3).reshape(areas, -1)
    system_diag = diag + capacity
    volt = start_volt
    hist = start_hist
    flat_ends = line_ends.reshape(areas, -1)
    for step in range(STEPS):
        rhs = sources[step] + capacity * volt
        rhs = jax.vmap(lambda r, e, h: r.at[e].add(-h))(rhs, flat_ends, hist.reshape(areas, -1))
        field = volt
        for sweep in range(SWEEPS):
            field = field + (rhs - product(blocks, pattern, field) - capacity * field) / system_diag
        volt = field
        end_volt = jax.vmap(lambda va, ea: va[ea])(volt, line_ends)
        message = -2.0 * surge * end_volt[:, 1] - hist[:, 1]
        new_left = jnp.roll(message, 1, axis=0)
        from_right_volt = jnp.roll(end_volt[:, 0], -1, axis=0)
        from_right_hist = jnp.roll(hist[:, 0], -1, axis=0)
        new_right = -2.0 * surge * from_right_volt - from_right_hist
        hist = jnp.stack([new_left, new_right], axis=1)
    return volt, hist
```

```python
import jax
import jax.numpy as jnp
from jax import lax
from jax.experimental import pallas as pl
from jax.experimental.pallas import tpu as pltpu
from jax.sharding import PartitionSpec as P

STEPS = 4
SWEEPS = 8
MESH = pl.DeviceIdType.MESH
SIDE = 4
SUBS = 16
ROWS = 64
WIDTH = 64
LANES = 128
SLOTS = 16
TILES = 8


def ring_distance(offset):
    return sum(min(part, SIDE - part) for part in divmod(offset, SIDE))


OFFSETS = sorted(range(1, SUBS), key=lambda offset: -ring_distance(offset))


def negated(offset):
    along_z, along_y = divmod(offset, SIDE)
    return (-along_z % SIDE) * SIDE + -along_y % SIDE


def lane_gather(values, index):
    return jnp.take_along_axis(values, index, axis=1, mode="promise_in_bounds")


def iota(axis, rows=8, columns=LANES):
    return lax.broadcasted_iota(jnp.int32, (rows, columns), axis)


def row_total(tile):
    for shift in (4, 2, 1):
        tile = tile + pltpu.roll(tile, shift, 0)
    return tile


def xor_mix(tiles):
    chunk = iota(1) // SLOTS
    for bit in (1, 2, 4):
        mask = (chunk & bit) != 0
        tiles = [jnp.where(mask, tiles[d ^ bit], tiles[d]) for d in range(TILES)]
    return tiles


def fold_rows(tiles):
    sub = iota(0)
    first = []
    for s in range(4):
        low = sub < 4
        kept = jnp.where(low, tiles[s], tiles[s + 4])
        moved = jnp.where(low, tiles[s + 4], tiles[s])
        first.append(kept + pltpu.roll(moved, 4, 0))
    low = (sub & 2) == 0
    second = [
        jnp.where(low, first[s] + pltpu.roll(first[s], 6, 0), first[s + 2] + pltpu.roll(first[s + 2], 2, 0))
        for s in range(2)
    ]
    low = (sub & 1) == 0
    return jnp.where(low, second[0] + pltpu.roll(second[0], 7, 0), second[1] + pltpu.roll(second[1], 1, 0))


def nt_dot(left, right, precision=None):
    return lax.dot_general(
        left, right, (((1,), (1,)), ((), ())), precision=precision, preferred_element_type=jnp.float32
    )


def nn_dot(left, right):
    return jnp.dot(left, right, preferred_element_type=jnp.float32)


def kernel(
    blocks, ints, vecs, lines, volt_out, hist_out,
    stage, turned, own, xs, ys, rhs, inverse, diag, hist_s, index, places,
    list_snd, list_rcv, snd, rcv, line_snd, line_rcv,
    stage_sem, list_ss, list_rs, ss, rs, line_ss, line_rs,
):
    area = lax.axis_index("area")
    areas = lax.axis_size("area")
    me = lax.axis_index("sub")
    my_z, my_y = me // SIDE, me % SIDE

    def peer(offset):
        along_z, along_y = divmod(offset, SIDE)
        return {"sub": ((my_z + along_z) % SIDE) * SIDE + (my_y + along_y) % SIDE}

    peers = {offset: peer(offset) for offset in OFFSETS}
    line_peers = ({"area": (area + 1) % areas}, {"area": (area + areas - 1) % areas})

    stage_copies = [
        pltpu.make_async_copy(blocks.at[:, pl.ds(LANES * half, LANES)], stage.at[half], stage_sem.at[half])
        for half in range(2)
    ]
    for copy in stage_copies:
        copy.start()

    barrier = pltpu.get_barrier_semaphore()
    for target in (*peers.values(), *line_peers):
        pl.semaphore_signal(barrier, inc=1, device_id=target, device_id_type=MESH)

    lane = iota(1)
    sub = iota(0)
    low_half = lane < WIDTH
    slot = lane % SLOTS

    pattern = [ints[0:1, :], ints[1:2, :]]
    groups = [p >> 6 for p in pattern]
    locals_ = [p & 63 for p in pattern]
    group_hot = [jnp.where(iota(0, LANES) == g, 1.0, 0.0) for g in groups]
    local_hot = [jnp.where(iota(0, ROWS) == l, 1.0, 0.0) for l in locals_]
    used = nt_dot(local_hot[0], group_hot[0]) + nt_dot(local_hot[1], group_hot[1])
    used = used > 0.5
    before = jnp.where(iota(1, ROWS, ROWS) < iota(0, ROWS, ROWS), 1.0, 0.0)
    rank = nn_dot(before, jnp.where(used, 1.0, 0.0))
    rank = jnp.where(used, rank, 99.0)
    spread = jnp.where(iota(0, LANES, 2 * LANES) == iota(1, LANES, 2 * LANES) // SLOTS, 1.0, 0.0)
    spread_rank = nn_dot(rank, spread)
    wanted = (iota(1, ROWS, 2 * LANES) % SLOTS).astype(jnp.float32)
    lists = jnp.sum(
        jnp.where(spread_rank == wanted, iota(0, ROWS, 2 * LANES).astype(jnp.float32), 0.0), axis=0, keepdims=True
    )
    list_snd[...] = jnp.where(
        sub < 4, jnp.broadcast_to(lists[:, :LANES], (8, LANES)), jnp.broadcast_to(lists[:, LANES:], (8, LANES))
    )

    pl.semaphore_wait(barrier, len(OFFSETS) + 2)

    for offset in OFFSETS:
        pltpu.make_async_remote_copy(
            src_ref=list_snd, dst_ref=list_rcv.at[offset], send_sem=list_ss, recv_sem=list_rs,
            device_id=peers[offset], device_id_type=MESH,
        ).start()

    for half in range(2):
        ranks = nn_dot(rank, group_hot[half])
        own_slot = jnp.sum(local_hot[half] * ranks, axis=0, keepdims=True).astype(jnp.int32)
        along_z = (my_z - (groups[half] >> 2) + SIDE) & 3
        along_y = (my_y - (groups[half] & 3) + SIDE) & 3
        offset = along_z * SIDE + along_y
        place = (offset & 7) * SLOTS + own_slot
        places[2 * half] = jnp.broadcast_to(place, (8, LANES))
        places[2 * half + 1] = jnp.broadcast_to(offset >> 3, (8, LANES))

    for tile in range(TILES):
        xs[tile] = vecs[STEPS + 1, pl.ds(8 * tile, 8), :]
    hist_s[...] = jnp.broadcast_to(lines[0:1, :], (8, LANES))
    list_all = pltpu.make_async_remote_copy(
        src_ref=list_rcv.at[pl.ds(1, SUBS - 1)], dst_ref=list_rcv.at[pl.ds(1, SUBS - 1)],
        send_sem=list_ss, recv_sem=list_rs, device_id=peers[1], device_id_type=MESH,
    )
    list_all.wait_recv()
    list_all.wait_send()
    bases = [jnp.zeros((8, LANES), jnp.int32) for _ in range(2)]
    my_chunk = (me % 8) * SLOTS + slot
    for offset in OFFSETS:
        to = negated(offset)
        row = list_rcv[offset, pl.ds((me // 8) * 4, 1), :]
        row = lane_gather(jnp.broadcast_to(row, (8, LANES)), my_chunk).astype(jnp.int32)
        bases[to // 8] = jnp.where(lane // SLOTS == to % 8, row, bases[to // 8])
    for tile in range(TILES):
        for high in range(2):
            index[2 * tile + high] = lane_gather(bases[high], lane ^ (tile * SLOTS))

    bus = ints[2:3, :] - me * (ROWS * WIDTH)
    inside = (bus >= 0) & (bus < ROWS * WIDTH)
    end_row = jnp.where(inside, bus >> 6, 0)
    end_at = jnp.where(inside, bus & 63, -1)

    def end_volts(x):
        total = jnp.zeros((8, LANES), jnp.float32)
        rows_of = jnp.broadcast_to(end_row, (8, LANES))
        for tile in range(TILES):
            total = total + jnp.where(sub + 8 * tile == end_at, lane_gather(x[tile], rows_of), 0.0)
        return row_total(total)

    def injection(hist):
        ends = jnp.where(iota(0, WIDTH) == end_at, jnp.broadcast_to(hist[0:1], (WIDTH, LANES)), 0.0)
        rows_hot = jnp.where((iota(0, LANES) % ROWS) == end_row, 1.0, 0.0)
        return nt_dot(ends, rows_hot, lax.Precision.HIGHEST)

    def send(q, x, end_tile=None):
        for high in range(2):
            mixed = xor_mix([lane_gather(x[tile], index[2 * tile + high]) for tile in range(TILES)])
            for d in range(TILES):
                if high * 8 + d:
                    out = mixed[d] if end_tile is None else jnp.where(slot >= 13, end_tile, mixed[d])
                    snd[q, high * 8 + d] = out
        for offset in OFFSETS:
            pltpu.make_async_remote_copy(
                src_ref=snd.at[q, offset], dst_ref=rcv.at[q, offset], send_sem=ss.at[q], recv_sem=rs.at[q],
                device_id=peers[offset], device_id_type=MESH,
            ).start()

    def arrived(q):
        everything = pltpu.make_async_remote_copy(
            src_ref=snd.at[q, pl.ds(1, SUBS - 1)], dst_ref=rcv.at[q, pl.ds(1, SUBS - 1)],
            send_sem=ss.at[q], recv_sem=rs.at[q], device_id=peers[1], device_id_type=MESH,
        )
        everything.wait_recv()
        everything.wait_send()

    def own_part(x):
        parts = [jnp.where(low_half, x[p], x[p + 4]) for p in range(4)]
        for i in range(WIDTH):
            total = turned[i, 12] * parts[0]
            for p in range(1, 4):
                total = total + turned[i, 12 + p] * parts[p]
            own[i] = total

    def remote_part(q):
        mixed = []
        for high in range(2):
            mixed.append(xor_mix([rcv[q, max(1, 8 * high + d)] for d in range(TILES)]))
        place, high = places[0], places[1] != 0
        picked = []
        for tile in range(TILES):
            at = place ^ (tile * SLOTS)
            picked.append(jnp.where(high, lane_gather(mixed[1][tile], at), lane_gather(mixed[0][tile], at)))
        place, high = places[2], places[3] != 0
        for tile in range(4):
            at = [place ^ ((tile + 4 * h) * SLOTS) for h in range(2)]
            both = [
                jnp.where(high, lane_gather(mixed[1][tile + 4 * h], at[h]), lane_gather(mixed[0][tile + 4 * h], at[h]))
                for h in range(2)
            ]
            picked.append(jnp.where(low_half, both[0], both[1]))
        for tile in range(TILES):
            totals = []
            for s in range(8):
                i = tile * 8 + s
                total = own[i]
                for p in range(12):
                    total = total + turned[i, p] * picked[p]
                totals.append(total)
            folded = fold_rows(totals)
            ys[tile] = folded + pltpu.roll(folded, WIDTH, 1)

    def capacity(tile):
        return vecs[STEPS, pl.ds(8 * tile, 8), :]

    send(1, [xs[tile] for tile in range(TILES)])

    for copy in stage_copies:
        copy.wait()

    def turn(i, carry):
        rows = [stage[half, pl.ds(i, ROWS, stride=WIDTH), :] for half in range(2)]
        out = jnp.concatenate(rows, axis=0).T
        tiles = [out[8 * p : 8 * p + 8] for p in range(16)]
        for p in range(8):
            turned[i, p] = tiles[8 + p]
        for p in range(4):
            a, b = tiles[p], tiles[p + 4]
            turned[i, 8 + p] = jnp.where(low_half, pltpu.roll(a, WIDTH, 1), b)
            turned[i, 12 + p] = jnp.where(low_half, a, pltpu.roll(b, WIDTH, 1))
        return carry

    lax.fori_loop(0, WIDTH, turn, 0)
    for tile in range(TILES):
        at = jnp.zeros((8, LANES), jnp.float32)
        for s in range(8):
            at = jnp.where(sub == s, turned[8 * tile + s, 12 + tile % 4], at)
        other = pltpu.roll(at, WIDTH, 1)
        diagonal = jnp.where(low_half, at, other) if tile < 4 else jnp.where(low_half, other, at)
        inverse[tile] = 1.0 / (diagonal + capacity(tile))

    own_part([xs[tile] for tile in range(TILES)])
    arrived(1)
    remote_part(1)

    def update():
        x = []
        for tile in range(TILES):
            old = xs[tile]
            new = old + (rhs[tile] - ys[tile] - capacity(tile) * old) * inverse[tile]
            xs[tile] = new
            x.append(new)
        return x

    end_index = sub * SLOTS + (lane // SLOTS) * 2 + jnp.clip(slot - 13, 0, 1)
    end_back = ((lane % SLOTS) // 2) * SLOTS + 13 + lane % 2
    surge = jnp.broadcast_to(lines[1:2, :], (8, LANES))

    def step(t, carry):
        hist = hist_s[...]
        inject = injection(hist)
        for tile in range(TILES):
            rhs[tile] = vecs[t, pl.ds(8 * tile, 8), :] + capacity(tile) * xs[tile] - inject[8 * tile : 8 * tile + 8]

        def sweep(s, inner):
            q = s % 2
            x = update()
            send(q, x)
            own_part(x)
            arrived(q)
            remote_part(q)
            return inner

        lax.fori_loop(0, SWEEPS - 1, sweep, 0)
        q = (SWEEPS - 1) % 2
        tq = t % 2
        x = update()
        end_tile = lane_gather(end_volts(x), end_index)
        send(q, x, end_tile)
        own_part(x)
        arrived(q)
        total = end_tile
        for offset in range(1, SUBS):
            total = total + rcv[q, offset]
        total = jnp.where(sub == lane // SLOTS, lane_gather(total, end_back), 0.0)
        ends = row_total(total)
        hist = hist_s[...]
        line_snd[tq, 0] = -2.0 * surge * ends - hist
        line_snd[tq, 1] = jnp.where(low_half, ends, pltpu.roll(hist, WIDTH, 1))
        copies = [
            pltpu.make_async_remote_copy(
                src_ref=line_snd.at[tq, way], dst_ref=line_rcv.at[tq, way],
                send_sem=line_ss.at[tq, way], recv_sem=line_rs.at[tq, way],
                device_id=line_peers[way], device_id_type=MESH,
            )
            for way in range(2)
        ]
        for copy in copies:
            copy.start()
        remote_part(q)
        for copy in copies:
            copy.wait()
        from_left, from_right = line_rcv[tq, 0], line_rcv[tq, 1]
        hist_s[...] = jnp.where(
            low_half, pltpu.roll(from_left, WIDTH, 1), -2.0 * surge * pltpu.roll(from_right, WIDTH, 1) - from_right
        )
        return carry

    lax.fori_loop(0, STEPS, step, 0)
    volt = jnp.concatenate([xs[tile] for tile in range(TILES)], axis=0)
    volt_out[...] = jnp.concatenate([volt, volt], axis=0).T[:ROWS, :WIDTH]
    hist_out[...] = hist_s[...]


def on_device(blocks, pattern, line_ends, sources, capacity, start_volt, start_hist, surge):
    vectors = jnp.concatenate([sources[:, 0], capacity, start_volt], axis=0).reshape(STEPS + 2, ROWS, WIDTH)
    vectors = jnp.swapaxes(vectors, 1, 2)
    vectors = jnp.concatenate([vectors, vectors], axis=2)
    columns = pattern[0].T
    ints = jnp.stack(
        [
            jnp.concatenate([columns[1], columns[3]]),
            jnp.concatenate([columns[2], columns[2]]),
            line_ends.reshape(LANES),
        ]
    )
    lines = jnp.stack([start_hist.reshape(LANES), jnp.concatenate([surge[0], surge[0]])])
    tile = (8, LANES)
    f32 = jnp.float32
    vmem = pl.BlockSpec(memory_space=pltpu.VMEM)
    volt, hist = pl.pallas_call(
        kernel,
        out_shape=(jax.ShapeDtypeStruct((ROWS, WIDTH), f32), jax.ShapeDtypeStruct(tile, f32)),
        in_specs=[pl.BlockSpec(memory_space=pl.ANY), vmem, vmem, vmem],
        out_specs=(vmem, vmem),
        scratch_shapes=[
            pltpu.VMEM((2, ROWS * WIDTH, LANES), f32),
            pltpu.VMEM((WIDTH, 16, *tile), f32),
            pltpu.VMEM((WIDTH, *tile), f32),
            pltpu.VMEM((TILES, *tile), f32),
            pltpu.VMEM((TILES, *tile), f32),
            pltpu.VMEM((TILES, *tile), f32),
            pltpu.VMEM((TILES, *tile), f32),
            pltpu.VMEM((TILES, *tile), f32),
            pltpu.VMEM(tile, f32),
            pltpu.VMEM((2 * TILES, *tile), jnp.int32),
            pltpu.VMEM((4, *tile), jnp.int32),
            pltpu.VMEM(tile, f32),
            pltpu.VMEM((SUBS, *tile), f32),
            pltpu.VMEM((2, SUBS, *tile), f32),
            pltpu.VMEM((2, SUBS, *tile), f32),
            pltpu.VMEM((2, 2, *tile), f32),
            pltpu.VMEM((2, 2, *tile), f32),
            pltpu.SemaphoreType.DMA((2,)),
            pltpu.SemaphoreType.DMA,
            pltpu.SemaphoreType.DMA,
            pltpu.SemaphoreType.DMA((2,)),
            pltpu.SemaphoreType.DMA((2,)),
            pltpu.SemaphoreType.DMA((2, 2)),
            pltpu.SemaphoreType.DMA((2, 2)),
        ],
        compiler_params=pltpu.CompilerParams(
            collective_id=0, has_side_effects=True, vmem_limit_bytes=32 * 2**20
        ),
    )(blocks.reshape(ROWS * WIDTH, 4 * WIDTH), ints, vectors, lines)
    return volt.reshape(1, ROWS * WIDTH), hist[0].reshape(1, 2, WIDTH)


def solution(mesh):
    in_specs = (
        P("area", "sub", None, None),
        P("area", "sub", None),
        P("area", None, None),
        P(None, "area", "sub"),
        P("area", "sub"),
        P("area", "sub"),
        P("area", None, None),
        P("area", None),
    )
    out_specs = (P("area", "sub"), P("area", None, None))
    return jax.shard_map(
        on_device, mesh=mesh, in_specs=in_specs, out_specs=out_specs, check_vma=False
    )
```
